512 devices in a mesh: section: 16 (over z), dp: 32 (over x, y, core).
Axes of the slice: x: 4, y: 4, z: 16, core: 2. Of those that a mesh axis runs over, the one named last changes fastest.
Arguments:
- gradients: bfloat16 [176, 288, 4096], P('section', None, 'dp'), may hold values from -210000 to 210000
- momentum: float32 [176, 288, 4096], P('section', None, 'dp'), may hold values from -60 to 60
Outputs:
- new_momentum: float32 [176, 288, 4096], P('section', None, 'dp')
- orthogonal_update: bfloat16 [176, 288, 4096], P('section', None, 'dp')
The draws below stay inside these ranges and needn't reach their ends.
All inputs are finite; a program needn't handle non-finite values.
Results may differ from the reference program's by a relative error of at most 0.0049.
Values may be sent and summed in bfloat16 or wider, within the bound.
A program may use at most 64 MiB of HBM per device.

```python
import math
import jax
import jax.numpy as jnp
from jax import lax

R = 288
D = 4096
ITERS = 2
MATS = 176


def scale_field(key, lower, upper, target_shape):
    return jnp.exp(jax.random.uniform(key, target_shape, jnp.float32, math.log(lower), math.log(upper)))


def draw_gradients(key, part):
    key = jax.random.fold_in(key, 11)
    key_list = jax.random.split(key, 8)
    full_shape = (MATS, R, D)
    row_scale = scale_field(key_list[1], 1.0, 10.0, (MATS, R, 1))
    column_scale = scale_field(key_list[2], 1.0, 10.0, (MATS, 1, D))
    layer_place = jnp.arange(MATS, dtype=jnp.float32)[:, None, None] / MATS
    column_place = jnp.arange(D, dtype=jnp.float32)[None, None, :] / D
    spike_mask = jax.random.bernoulli(key_list[4], 1.0 / 256.0, full_shape).astype(jnp.float32)
    spike_size = 13.8 * scale_field(key_list[5], 1.0, 4.0, full_shape)
    noise_field = jnp.clip(jax.random.normal(key_list[0], full_shape, jnp.float32), -6.0, 6.0)
    spike_noise = jnp.clip(jax.random.normal(key_list[6], full_shape, jnp.float32), -6.0, 6.0)
    ramp_scale = jnp.exp(0.5 * math.log(3.0) * (layer_place + column_place))
    global_factor = scale_field(key_list[7], 0.25, 2.0, (1, 1, 1))
    combined = noise_field + spike_mask * spike_size * spike_noise
    return (combined * row_scale * column_scale * ramp_scale * global_factor).astype(jnp.bfloat16)


def draw_momentum(key, part):
    key = jax.random.fold_in(key, 23)
    key_list = jax.random.split(key, 3)
    full_shape = (MATS, R, D)
    row_scale = scale_field(key_list[1], 0.3, 3.0, (MATS, R, 1))
    column_scale = scale_field(key_list[2], 0.3, 3.0, (MATS, 1, D))
    noise_field = jnp.clip(jax.random.normal(key_list[0], full_shape, jnp.float32), -6.0, 6.0)
    return (noise_field * row_scale * column_scale).astype(jnp.float32)


def setup_inputs(seed: int = 0) -> dict:
    streams_of = jax.random.split(jax.random.key(seed), 3)
    gradients = draw_gradients(jax.random.fold_in(streams_of[2], 71), 0)
    momentum = draw_momentum(jax.random.fold_in(streams_of[2], 71), 0)
    return {"gradients": gradients, "momentum": momentum}


momentum_decay = 0.95
quintic_one = 3.4445
quintic_two = -4.775
quintic_three = 2.0315

def orthogonalize(prepared, width_scale):
    values = prepared.astype(jnp.float32)
    norm_value = jnp.sqrt(jnp.sum(values * values))
    matrix = values / (norm_value + 1e-07)
    for sweep_index in range(ITERS):
        gram_mat = jnp.dot(matrix, matrix.T, precision=lax.Precision.HIGHEST, preferred_element_type=jnp.float32)
        squared = jnp.dot(gram_mat, gram_mat, precision=lax.Precision.HIGHEST, preferred_element_type=jnp.float32)
        poly_mat = quintic_two * gram_mat + quintic_three * squared
        matrix = quintic_one * matrix + jnp.dot(poly_mat, matrix, precision=lax.Precision.HIGHEST, preferred_element_type=jnp.float32)
    return (width_scale * matrix).astype(jnp.bfloat16)

def reference(gradients, momentum):
    total = jnp.sum(jnp.square(gradients.astype(jnp.float32)))
    entries = gradients.shape[0] * gradients.shape[1] * gradients.shape[2]
    clip_factor = jnp.minimum(1.0, lax.rsqrt(total / entries + 1e-06))
    width_scale = math.sqrt(max(gradients.shape[1], gradients.shape[2]))

    def per_matrix(pair_in):
        grad_one, moment_one = pair_in
        scaled = grad_one.astype(jnp.float32) * clip_factor
        moment_new = momentum_decay * moment_one + scaled
        prepared = (scaled + momentum_decay * moment_new).astype(jnp.bfloat16)
        return (moment_new, orthogonalize(prepared, width_scale))
    new_momentum, orthogonal_update = lax.map(per_matrix, (gradients, momentum))
    return (new_momentum, orthogonal_update)
```

```python
import jax
import jax.numpy as jnp
from jax import lax
from jax.experimental import pallas as pl
from jax.experimental.pallas import tpu as pltpu
from jax.sharding import PartitionSpec as P

MATS = 11
ROWS = 288
COLS = 128
HALF = 6
PACK = 352
PART = 176
ENTRIES = 176 * 288 * 4096
WIDTH_SCALE = 64.0

DECAY = 0.95
ONE = 3.4445
TWO = -4.775
THREE = 2.0315

F32 = jnp.float32
BF16 = jnp.bfloat16
MESH = pl.DeviceIdType.MESH


def dot(a, b):
    return jnp.dot(a, b, preferred_element_type=F32)


def dot_nt(a, b):
    return lax.dot_general(a, b, (((1,), (1,)), ((), ())), preferred_element_type=F32)


def split(a):
    high = a.astype(BF16)
    return high, (a - high.astype(F32)).astype(BF16)


def product(a, b):
    wide, tail = slice(0, 256), slice(256, 288)
    left = jnp.concatenate(
        [a[0][:, wide], a[0][:, wide], a[1][:, wide], a[0][:, tail], a[0][:, tail], a[1][:, tail]], axis=1
    )
    right = jnp.concatenate([b[0][wide], b[1][wide], b[0][wide], b[0][tail], b[1][tail], b[0][tail]], axis=0)
    main = dot(left, right[:, wide])
    corner = dot(left[tail], right[:, tail])
    side = jnp.concatenate([main[tail].T, corner], axis=0)
    return jnp.concatenate([main, side], axis=1)


def triangle():
    row = lax.broadcasted_iota(jnp.int32, (128, 128), 0)
    col = lax.broadcasted_iota(jnp.int32, (128, 128), 1)
    return row, col


def pack(first, cross, second, low):
    row, col = triangle()
    middle = jnp.sum(jnp.where(row == col, second, 0.0), axis=0, keepdims=True)
    rest = jnp.concatenate([middle[:, 96:128], jnp.zeros((1, 64), F32)], axis=1)
    beside = jnp.concatenate(
        [jnp.broadcast_to(middle[:, 0:96], (16, 96)), jnp.broadcast_to(rest, (16, 96))], axis=0
    )
    corner = jnp.concatenate([low[:, 256:288], beside], axis=1)
    return (
        (0, jnp.where(col >= row, first, second)),
        (128, cross),
        (256, low[:, :128]),
        (288, low[:, 128:256]),
        (320, corner),
    )


def unpack(full, both, cross, low0, low1, corner):
    row, col = triangle()
    middle = jnp.concatenate([corner[0:1, 32:128], corner[16:17, 32:64]], axis=1)
    turned = both.T
    low = jnp.concatenate([low0, low1], axis=1)
    full[0:128, 0:128] = jnp.where(col >= row, both, turned)
    full[0:128, 128:256] = cross
    full[128:256, 0:128] = cross.T
    full[128:256, 128:256] = jnp.where(
        row == col, jnp.broadcast_to(middle, (128, 128)), jnp.where(row > col, both, turned)
    )
    full[256:288, 0:256] = low
    full[0:256, 256:288] = low.T
    full[256:288, 256:288] = corner[:, :32]


def kernel(
    g_hbm,
    m_hbm,
    nm_out,
    o_hbm,
    gbuf,
    mbuf,
    nmbuf,
    acc,
    accz,
    accp,
    gx,
    mx,
    xx,
    gloc,
    gtx,
    r1,
    s2,
    r2,
    gf,
    qbuf,
    obuf,
    g_sem,
    m_sem,
    nm_sem,
    z_send,
    z_recv,
    p_send,
    p_recv,
    x_send,
    x_recv,
    mx_send,
    mx_recv,
    s1_send,
    s1_recv,
    s2_send,
    s2_recv,
    q1_send,
    q2_send,
    q_recv,
    o_send,
    o_recv,
    ol_sem,
    relay,
):
    z = lax.axis_index("section")
    d = lax.axis_index("dp")
    x = d // 8
    y = (d // 2) % 4
    c = d % 2

    def dev(px, py, pc):
        return (z, (px * 4 + py) * 2 + pc)

    partner = dev(x, y, 1 - c)

    def remote(src, dst, send, recv, target):
        return pltpu.make_async_remote_copy(
            src_ref=src, dst_ref=dst, send_sem=send, recv_sem=recv, device_id=target, device_id_type=MESH
        )

    def load_g(i):
        return pltpu.make_async_copy(g_hbm.at[i], gbuf.at[i], g_sem.at[i])

    def store_nm(i):
        return pltpu.make_async_copy(nmbuf.at[i], nm_out.at[i], nm_sem.at[i])

    def load_m(i):
        return pltpu.make_async_copy(m_hbm.at[i], mbuf.at[i], m_sem.at[i])

    @pl.loop(0, MATS)
    def _(i):
        load_g(i).start()

    barrier = pltpu.get_barrier_semaphore()

    def greet(target):
        pl.semaphore_signal(barrier, inc=1, device_id=target, device_id_type=MESH)

    @pl.loop(1, 5)
    def _(o):
        greet((lax.rem(z + o, 16), d))
        greet((lax.rem(z + 16 - o, 16), d))

    @pl.loop(1, 16)
    def _(o):
        greet(dev((x + o // 4) % 4, (y + o) % 4, c))

    greet(partner)

    def squares(i, total):
        load_g(i).wait()
        value = gbuf[i].astype(F32)
        return total + jnp.sum((value * value).reshape(ROWS // 8, 8, COLS), axis=0)

    total = lax.fori_loop(0, MATS, squares, jnp.zeros((8, COLS), F32))
    acc[0, 0:1] = jnp.sum(total, axis=0, keepdims=True)

    @pl.loop(0, MATS)
    def _(i):
        load_m(i).start()

    pl.semaphore_wait(barrier, 24)

    pl.semaphore_signal(relay.at[0], inc=1, device_id=(lax.rem(z + 4, 16), d), device_id_type=MESH)
    pl.semaphore_signal(relay.at[1], inc=1, device_id=(lax.rem(z + 12, 16), d), device_id_type=MESH)

    def core_copy():
        return remote(
            acc.at[0, pl.ds(0, 1)], accp.at[15, pl.ds(0, 1)], p_send.at[15], p_recv.at[15], partner
        )

    core_copy().start()
    core_copy().wait_recv()
    acc[1, 0:1] = acc[0, 0:1] + accp[15, 0:1]

    def p_copy(o):
        return remote(
            acc.at[1, pl.ds(0, 1)],
            accp.at[o - 1, pl.ds(0, 1)],
            p_send.at[o - 1],
            p_recv.at[o - 1],
            dev((x + o // 4) % 4, (y + o) % 4, c),
        )

    @pl.loop(1, 16)
    def _(o):
        p_copy(o).start()

    def gx_copy(j):
        return remote(gbuf.at[HALF * (1 - c) + j], gx.at[j], x_send.at[j], x_recv.at[j], partner)

    def mx_copy(j):
        return remote(mbuf.at[HALF * (1 - c) + j], mx.at[j], mx_send.at[j], mx_recv.at[j], partner)

    @pl.loop(0, MATS)
    def _(i):
        load_m(i).wait()

    @pl.loop(0, HALF)
    def _(j):
        @pl.when(HALF * (1 - c) + j < MATS)
        def _():
            gx_copy(j).start()
            mx_copy(j).start()

    pl.semaphore_wait(relay.at[0], 1)
    pl.semaphore_wait(relay.at[1], 1)

    @pl.loop(1, 16)
    def _(o):
        p_copy(o).wait_recv()

    acc[2, 0:1] = acc[1, 0:1] + jnp.sum(accp[0:15, 0:1, :], axis=0)

    def z_copy(o):
        return remote(
            acc.at[2, pl.ds(0, 1)],
            accz.at[o - 1, pl.ds(0, 1)],
            z_send.at[o - 1],
            z_recv.at[o - 1],
            (lax.rem(z + o, 16), d),
        )

    @pl.loop(1, 16)
    def _(o):
        z_copy(o).start()

    @pl.loop(1, 16)
    def _(o):
        z_copy(o).wait_recv()

    mean = jnp.sum(acc[2, 0:1] + jnp.sum(accz[:, 0:1, :], axis=0), keepdims=True) / ENTRIES + 1e-06
    root = lax.rsqrt(mean)
    root = root * (1.5 - 0.5 * mean * root * root)
    clip = jnp.minimum(1.0, root)

    def prepare(gradient, moment):
        scaled = gradient.astype(F32) * clip
        return (scaled + DECAY * (DECAY * moment + scaled)).astype(BF16)

    def owner(j):
        m = HALF * c + j
        return m < MATS, m % 4, (m // 4 + m % 4) % 4

    def slot(own, at):
        return jnp.maximum((own - at + 4) % 4 - 1, 0)

    def scale(px, py):
        return jnp.broadcast_to((16 + px * 4 + py).astype(F32) * 0.0625, (1, COLS))

    def s1_x(j, xm):
        k = slot(x, xm)
        return remote(
            gtx.at[j, pl.ds(0, PART)], r1.at[0, j, k], s1_send.at[0, j], s1_recv.at[0, j, k], dev(xm, y, c)
        )

    def s1_y(j, ym):
        k = slot(y, ym)
        return remote(
            gtx.at[j, pl.ds(PART, PART)], r1.at[1, j, k], s1_send.at[1, j], s1_recv.at[1, j, k], dev(x, ym, c)
        )

    @pl.loop(0, HALF)
    def _(j):
        real, xm, ym = owner(j)

        @pl.when(real)
        def _():
            m = HALF * c + j
            remote(gx.at[j], gx.at[j], x_send.at[j], x_recv.at[j], partner).wait_recv()
            remote(mx.at[j], mx.at[j], mx_send.at[j], mx_recv.at[j], partner).wait_recv()
            xx[j, 0] = prepare(gbuf[m], mbuf[m])
            xx[j, 1] = prepare(gx[j], mx[j])
            value = jnp.concatenate([xx[j, 0], xx[j, 1]], axis=1)
            top = dot_nt(value[:128], value[:256])
            mid = dot_nt(value[128:256], value[128:256])
            low = dot_nt(value[256:288], value)
            pieces = pack(top[:, :128], top[:, 128:], mid, low)
            own_scale = scale(x, y)
            for at, piece in pieces:
                gloc[j, at : at + piece.shape[0]] = piece
                gtx[j, at : at + piece.shape[0]] = (piece * own_scale).astype(BF16)

            @pl.when(xm != x)
            def _():
                s1_x(j, xm).start()

            @pl.when(ym != y)
            def _():
                s1_y(j, ym).start()

    @pl.loop(0, MATS)
    def _(i):
        nmbuf[i] = DECAY * mbuf[i] + gbuf[i].astype(F32) * clip
        store_nm(i).start()

    def s2_x(j, ym):
        k = slot(y, ym)
        return remote(s2.at[0, j], r2.at[0, k], s2_send.at[0, j], s2_recv.at[0, k], dev(x, ym, c))

    def s2_y(j, xm):
        k = slot(x, xm)
        return remote(s2.at[1, j], r2.at[1, k], s2_send.at[1, j], s2_recv.at[1, k], dev(xm, y, c))

    def wait_r1(half, j, k):
        remote(r1.at[half, j, k], r1.at[half, j, k], s1_send.at[half, j], s1_recv.at[half, j, k], partner).wait_recv()

    def wait_r2(half, k):
        remote(r2.at[half, k], r2.at[half, k], s2_send.at[half, 0], s2_recv.at[half, k], partner).wait_recv()

    @pl.loop(0, HALF)
    def _(j):
        real, xm, ym = owner(j)

        def reduce(half, near, far, start):
            @pl.when(real & near)
            def _():
                for k in range(3):
                    wait_r1(half, j, k)
                total = gloc[j, PART * half : PART * half + PART]
                for k in range(3):
                    from_x = (x + k + 1) % 4 if half == 0 else x
                    from_y = y if half == 0 else (y + k + 1) % 4
                    total = total + r1[half, j, k].astype(F32) * (1.0 / scale(from_x, from_y))
                gloc[j, PART * half : PART * half + PART] = total

                @pl.when(far)
                def _():
                    s2[half, j] = (total * scale(x, y)).astype(BF16)
                    start()

        reduce(0, xm == x, ym != y, lambda: s2_x(j, ym).start())
        reduce(1, ym == y, xm != x, lambda: s2_y(j, xm).start())

    def q1_copy(j, half, k, o):
        target = dev(x, (y + o) % 4, c) if half == 0 else dev((x + o) % 4, y, c)
        return remote(
            qbuf.at[j, half, k], qbuf.at[j, half, k], q1_send.at[half, k, o - 1], q_recv.at[j, half, k], target
        )

    def q2_copy(j, half, k, o):
        target = dev((x + o) % 4, y, c) if half == 0 else dev(x, (y + o) % 4, c)
        return remote(
            qbuf.at[j, half, k], qbuf.at[j, half, k], q2_send.at[j, half, k, o - 1], q_recv.at[j, half, k], target
        )

    @pl.loop(0, HALF)
    def _(j):
        real, xm, ym = owner(j)

        @pl.when(real & (xm == x) & (ym == y))
        def _():
            for half in range(2):
                for k in range(3):
                    wait_r2(half, k)
                total = gloc[j, PART * half : PART * half + PART]
                for k in range(3):
                    from_x = x if half == 0 else (x + k + 1) % 4
                    from_y = (y + k + 1) % 4 if half == 0 else y
                    total = total + r2[half, k].astype(F32) * (1.0 / scale(from_x, from_y))
                gloc[j, PART * half : PART * half + PART] = total
            unpack(
                gf,
                gloc[j, 0:128],
                gloc[j, 128:256],
                gloc[j, 256:288],
                gloc[j, 288:320],
                gloc[j, 320:352],
            )
            row = lax.broadcasted_iota(jnp.int32, (ROWS, ROWS), 0)
            col = lax.broadcasted_iota(jnp.int32, (ROWS, ROWS), 1)
            diag = row == col
            raw = gf[...]
            norm = jnp.sqrt(jnp.sum(jnp.where(diag, raw, 0.0), keepdims=True)) + 1e-07
            inverse = 1.0 / norm
            gram = raw * (inverse * inverse)
            gram_s = split(gram)
            poly = TWO * gram + THREE * product(gram_s, gram_s) + jnp.where(diag, ONE, 0.0)
            poly_s = split(poly)
            left_s = split(product(poly_s, gram_s))
            gram = product(left_s, poly_s)
            gram_s = split(gram)
            last = TWO * gram + THREE * product(gram_s, gram_s) + jnp.where(diag, ONE, 0.0)
            gf[...] = product(split(last), poly_s) * (WIDTH_SCALE * inverse)

            pieces = pack(gf[0:128, 0:128], gf[0:128, 128:256], gf[128:256, 128:256], gf[256:288, :])
            for at, piece in pieces:
                both = split(piece)
                size = piece.shape[0]
                for half in range(2):
                    lo = max(at, PART * half)
                    hi = min(at + size, PART * half + PART)
                    if lo < hi:
                        for k in range(2):
                            qbuf[j, half, k, lo - PART * half : hi - PART * half] = both[k][lo - at : hi - at]
            for k in range(2):
                for half in range(2):
                    for o in (2, 1, 3):
                        q1_copy(j, half, k, o).start()

    def wait_q(j, half, k):
        remote(
            qbuf.at[j, half, k], qbuf.at[j, half, k], q1_send.at[half, k, 0], q_recv.at[j, half, k], partner
        ).wait_recv()

    @pl.loop(0, HALF)
    def _(j):
        real, xm, ym = owner(j)

        def forward(half, k, near, far):
            @pl.when(real & near)
            def _():
                @pl.when(far)
                def _():
                    wait_q(j, half, k)

                for o in (2, 1, 3):
                    q2_copy(j, half, k, o).start()

        for k in range(2):
            forward(0, k, xm == x, ym != y)
            forward(1, k, ym == y, xm != x)

    @pl.loop(0, MATS)
    def _(i):
        store_nm(i).wait()

    @pl.loop(1, 16)
    def _(o):
        z_copy(o).wait_send()
        p_copy(o).wait_send()

    core_copy().wait_send()

    @pl.loop(0, HALF)
    def _(j):
        real, xm, ym = owner(j)

        @pl.when(HALF * (1 - c) + j < MATS)
        def _():
            gx_copy(j).wait_send()
            mx_copy(j).wait_send()

        @pl.when(real)
        def _():
            @pl.when(xm != x)
            def _():
                s1_x(j, xm).wait_send()

            @pl.when(ym != y)
            def _():
                s1_y(j, ym).wait_send()

            @pl.when((xm == x) & (ym != y))
            def _():
                s2_x(j, ym).wait_send()

            @pl.when((ym == y) & (xm != x))
            def _():
                s2_y(j, xm).wait_send()

    def o_copy(j):
        m = HALF * c + j
        return remote(obuf.at[j, 1], o_hbm.at[m], o_send.at[j], o_recv.at[j], partner)

    def o_local(j):
        m = HALF * c + j
        return pltpu.make_async_copy(obuf.at[j, 0], o_hbm.at[m], ol_sem.at[j])

    @pl.loop(0, HALF)
    def _(j):
        real, xm, ym = owner(j)

        @pl.when(real)
        def _():
            @pl.when(xm != x)
            def _():
                wait_q(j, 0, 0)
                wait_q(j, 0, 1)

            @pl.when(ym != y)
            def _():
                wait_q(j, 1, 0)
                wait_q(j, 1, 1)

            first = qbuf[j, 0, 0].astype(F32) + qbuf[j, 0, 1].astype(F32)
            second = qbuf[j, 1, 0].astype(F32) + qbuf[j, 1, 1].astype(F32)
            cross = jnp.concatenate([first[128:176], second[0:80]], axis=0)
            unpack(gf, first[0:128], cross, second[80:112], second[112:144], second[144:176])
            full = split(gf[...])
            value = jnp.concatenate([xx[j, 0], xx[j, 1]], axis=1)
            result = (dot(full[0], value) + dot(full[1], value)).astype(BF16)
            obuf[j, 0] = result[:, :128]
            obuf[j, 1] = result[:, 128:]
            o_local(j).start()
            o_copy(j).start()

    @pl.loop(0, HALF)
    def _(j):
        real, xm, ym = owner(j)

        @pl.when(real & (xm == x) & (ym == y))
        def _():
            for k in range(2):
                for half in range(2):
                    for o in range(1, 4):
                        q1_copy(j, half, k, o).wait_send()

        @pl.when(real & (xm == x))
        def _():
            for k in range(2):
                for o in range(1, 4):
                    q2_copy(j, 0, k, o).wait_send()

        @pl.when(real & (ym == y))
        def _():
            for k in range(2):
                for o in range(1, 4):
                    q2_copy(j, 1, k, o).wait_send()

    @pl.loop(0, HALF)
    def _(j):
        @pl.when(HALF * (1 - c) + j < MATS)
        def _():
            remote(obuf.at[j, 1], obuf.at[j, 1], o_send.at[j], o_recv.at[j], partner).wait_recv()

        @pl.when(HALF * c + j < MATS)
        def _():
            o_local(j).wait()
            o_copy(j).wait_send()


def per_device(gradients, momentum):
    dma = pltpu.SemaphoreType.DMA
    vmem = pltpu.VMEM
    any_spec = pl.BlockSpec(memory_space=pl.ANY)
    return pl.pallas_call(
        kernel,
        out_shape=(
            jax.ShapeDtypeStruct((MATS, ROWS, COLS), F32),
            jax.ShapeDtypeStruct((MATS, ROWS, COLS), BF16),
        ),
        in_specs=[pl.BlockSpec(memory_space=pltpu.HBM)] * 2,
        out_specs=(any_spec, any_spec),
        scratch_shapes=[
            vmem((MATS, ROWS, COLS), BF16),
            vmem((MATS, ROWS, COLS), F32),
            vmem((MATS, ROWS, COLS), F32),
            vmem((3, 8, COLS), F32),
            vmem((15, 8, COLS), F32),
            vmem((16, 8, COLS), F32),
            vmem((HALF, ROWS, COLS), BF16),
            vmem((HALF, ROWS, COLS), F32),
            vmem((HALF, 2, ROWS, COLS), BF16),
            vmem((HALF, PACK, COLS), F32),
            vmem((HALF, PACK, COLS), BF16),
            vmem((2, HALF, 3, PART, COLS), BF16),
            vmem((2, HALF, PART, COLS), BF16),
            vmem((2, 3, PART, COLS), BF16),
            vmem((ROWS, ROWS), F32),
            vmem((HALF, 2, 2, PART, COLS), BF16),
            vmem((HALF, 2, ROWS, COLS), BF16),
            dma((MATS,)),
            dma((MATS,)),
            dma((MATS,)),
            dma((15,)),
            dma((15,)),
            dma((16,)),
            dma((16,)),
            dma((HALF,)),
            dma((HALF,)),
            dma((HALF,)),
            dma((HALF,)),
            dma((2, HALF)),
            dma((2, HALF, 3)),
            dma((2, HALF)),
            dma((2, 3)),
            dma((2, 2, 3)),
            dma((HALF, 2, 2, 3)),
            dma((HALF, 2, 2)),
            dma((HALF,)),
            dma((HALF,)),
            dma((HALF,)),
            pltpu.SemaphoreType.REGULAR((2,)),
        ],
        compiler_params=pltpu.CompilerParams(
            collective_id=0, has_side_effects=True, vmem_limit_bytes=40 * 1024 * 1024
        ),
        cost_estimate=pl.CostEstimate(flops=1500000000, bytes_accessed=5000000, transcendentals=0),
        name="muon",
    )(
        pltpu.with_memory_space_constraint(gradients, pltpu.HBM),
        pltpu.with_memory_space_constraint(momentum, pltpu.HBM),
    )


def solution(mesh):
    placed = (P("section", None, "dp"), P("section", None, "dp"))
    return jax.shard_map(
        per_device, mesh=mesh, in_specs=placed, out_specs=placed, check_vma=False
    )
```

```python
import jax
import jax.numpy as jnp
from jax import lax
from jax.experimental import pallas as pl
from jax.experimental.pallas import tpu as pltpu
from jax.sharding import PartitionSpec as P

MATS = 11
ROWS = 288
COLS = 128
HALF = 6
PACK = 352
PART = 176
ENTRIES = 176 * 288 * 4096
WIDTH_SCALE = 64.0

DECAY = 0.95
ONE = 3.4445
TWO = -4.775
THREE = 2.0315

F32 = jnp.float32
BF16 = jnp.bfloat16
MESH = pl.DeviceIdType.MESH


def dot(a, b):
    return jnp.dot(a, b, preferred_element_type=F32)


def dot_nt(a, b):
    return lax.dot_general(a, b, (((1,), (1,)), ((), ())), preferred_element_type=F32)


def split(a):
    high = a.astype(BF16)
    return high, (a - high.astype(F32)).astype(BF16)


def product(a, b):
    wide, tail = slice(0, 256), slice(256, 288)
    left = jnp.concatenate(
        [a[0][:, wide], a[0][:, wide], a[1][:, wide], a[0][:, tail], a[0][:, tail], a[1][:, tail]], axis=1
    )
    right = jnp.concatenate([b[0][wide], b[1][wide], b[0][wide], b[0][tail], b[1][tail], b[0][tail]], axis=0)
    main = dot(left, right[:, wide])
    corner = dot(left[tail], right[:, tail])
    side = jnp.concatenate([main[tail].T, corner], axis=0)
    return jnp.concatenate([main, side], axis=1)


def triangle():
    row = lax.broadcasted_iota(jnp.int32, (128, 128), 0)
    col = lax.broadcasted_iota(jnp.int32, (128, 128), 1)
    return row, col


def pack(first, cross, second, low):
    row, col = triangle()
    middle = jnp.sum(jnp.where(row == col, second, 0.0), axis=0, keepdims=True)
    rest = jnp.concatenate([middle[:, 96:128], jnp.zeros((1, 64), F32)], axis=1)
    beside = jnp.concatenate(
        [jnp.broadcast_to(middle[:, 0:96], (16, 96)), jnp.broadcast_to(rest, (16, 96))], axis=0
    )
    corner = jnp.concatenate([low[:, 256:288], beside], axis=1)
    return (
        (0, jnp.where(col >= row, first, second)),
        (128, cross),
        (256, low[:, :128]),
        (288, low[:, 128:256]),
        (320, corner),
    )


def unpack(full, both, cross, low0, low1, corner):
    row, col = triangle()
    middle = jnp.concatenate([corner[0:1, 32:128], corner[16:17, 32:64]], axis=1)
    turned = both.T
    low = jnp.concatenate([low0, low1], axis=1)
    full[0:128, 0:128] = jnp.where(col >= row, both, turned)
    full[0:128, 128:256] = cross
    full[128:256, 0:128] = cross.T
    full[128:256, 128:256] = jnp.where(
        row == col, jnp.broadcast_to(middle, (128, 128)), jnp.where(row > col, both, turned)
    )
    full[256:288, 0:256] = low
    full[0:256, 256:288] = low.T
    full[256:288, 256:288] = corner[:, :32]


def kernel(
    g_hbm,
    m_hbm,
    nm_out,
    o_hbm,
    gbuf,
    mbuf,
    nmbuf,
    acc,
    accz,
    accp,
    gx,
    mx,
    xx,
    gloc,
    gtx,
    r1,
    s2,
    r2,
    gf,
    qbuf,
    obuf,
    g_sem,
    m_sem,
    nm_sem,
    z_send,
    z_recv,
    p_send,
    p_recv,
    x_send,
    x_recv,
    mx_send,
    mx_recv,
    s1_send,
    s1_recv,
    s2_send,
    s2_recv,
    q1_send,
    q2_send,
    q_recv,
    o_send,
    o_recv,
    ol_sem,
    relay,
):
    z = lax.axis_index("section")
    d = lax.axis_index("dp")
    x = d // 8
    y = (d // 2) % 4
    c = d % 2

    def dev(px, py, pc):
        return (z, (px * 4 + py) * 2 + pc)

    partner = dev(x, y, 1 - c)

    def remote(src, dst, send, recv, target):
        return pltpu.make_async_remote_copy(
            src_ref=src, dst_ref=dst, send_sem=send, recv_sem=recv, device_id=target, device_id_type=MESH
        )

    def load_g(i):
        return pltpu.make_async_copy(g_hbm.at[i], gbuf.at[i], g_sem.at[i])

    def store_nm(i):
        return pltpu.make_async_copy(nmbuf.at[i], nm_out.at[i], nm_sem.at[i])

    def load_m(i):
        return pltpu.make_async_copy(m_hbm.at[i], mbuf.at[i], m_sem.at[i])

    @pl.loop(0, MATS)
    def _(i):
        load_g(i).start()

    barrier = pltpu.get_barrier_semaphore()

    def greet(target):
        pl.semaphore_signal(barrier, inc=1, device_id=target, device_id_type=MESH)

    @pl.loop(1, 5)
    def _(o):
        greet((lax.rem(z + o, 16), d))
        greet((lax.rem(z + 16 - o, 16), d))

    @pl.loop(1, 16)
    def _(o):
        greet(dev((x + o // 4) % 4, (y + o) % 4, c))

    greet(partner)

    def squares(i, total):
        load_g(i).wait()
        value = gbuf[i].astype(F32)
        return total + jnp.sum((value * value).reshape(ROWS // 8, 8, COLS), axis=0)

    total = lax.fori_loop(0, MATS, squares, jnp.zeros((8, COLS), F32))
    acc[0, 0:1] = jnp.sum(total, axis=0, keepdims=True)

    @pl.loop(0, MATS)
    def _(i):
        load_m(i).start()

    pl.semaphore_wait(barrier, 24)

    pl.semaphore_signal(relay.at[0], inc=1, device_id=(lax.rem(z + 4, 16), d), device_id_type=MESH)
    pl.semaphore_signal(relay.at[1], inc=1, device_id=(lax.rem(z + 12, 16), d), device_id_type=MESH)

    def core_copy():
        return remote(
            acc.at[0, pl.ds(0, 1)], accp.at[15, pl.ds(0, 1)], p_send.at[15], p_recv.at[15], partner
        )

    core_copy().start()
    core_copy().wait_recv()
    acc[1, 0:1] = acc[0, 0:1] + accp[15, 0:1]

    def p_copy(o):
        return remote(
            acc.at[1, pl.ds(0, 1)],
            accp.at[o - 1, pl.ds(0, 1)],
            p_send.at[o - 1],
            p_recv.at[o - 1],
            dev((x + o // 4) % 4, (y + o) % 4, c),
        )

    @pl.loop(1, 16)
    def _(o):
        p_copy(o).start()

    def gx_copy(j):
        return remote(gbuf.at[HALF * (1 - c) + j], gx.at[j], x_send.at[j], x_recv.at[j], partner)

    def mx_copy(j):
        return remote(mbuf.at[HALF * (1 - c) + j], mx.at[j], mx_send.at[j], mx_recv.at[j], partner)

    @pl.loop(0, MATS)
    def _(i):
        load_m(i).wait()

    @pl.loop(0, HALF)
    def _(j):
        @pl.when(HALF * (1 - c) + j < MATS)
        def _():
            gx_copy(j).start()
            mx_copy(j).start()

    pl.semaphore_wait(relay.at[0], 1)
    pl.semaphore_wait(relay.at[1], 1)

    @pl.loop(1, 16)
    def _(o):
        p_copy(o).wait_recv()

    acc[2, 0:1] = acc[1, 0:1] + jnp.sum(accp[0:15, 0:1, :], axis=0)

    def z_copy(o):
        return remote(
            acc.at[2, pl.ds(0, 1)],
            accz.at[o - 1, pl.ds(0, 1)],
            z_send.at[o - 1],
            z_recv.at[o - 1],
            (lax.rem(z + o, 16), d),
        )

    @pl.loop(1, 16)
    def _(o):
        z_copy(o).start()

    @pl.loop(1, 16)
    def _(o):
        z_copy(o).wait_recv()

    mean = jnp.sum(acc[2, 0:1] + jnp.sum(accz[:, 0:1, :], axis=0), keepdims=True) / ENTRIES + 1e-06
    root = lax.rsqrt(mean)
    root = root * (1.5 - 0.5 * mean * root * root)
    clip = jnp.minimum(1.0, root)

    def prepare(gradient, moment):
        scaled = gradient.astype(F32) * clip
        return (scaled + DECAY * (DECAY * moment + scaled)).astype(BF16)

    def owner(j):
        m = HALF * c + j
        return m < MATS, m % 4, (m // 4 + m % 4) % 4

    def slot(own, at):
        return jnp.maximum((own - at + 4) % 4 - 1, 0)

    def scale(px, py):
        return jnp.broadcast_to((16 + px * 4 + py).astype(F32) * 0.0625, (1, COLS))

    def s1_x(j, xm):
        k = slot(x, xm)
        return remote(
            gtx.at[j, pl.ds(0, PART)], r1.at[0, j, k], s1_send.at[0, j], s1_recv.at[0, j, k], dev(xm, y, c)
        )

    def s1_y(j, ym):
        k = slot(y, ym)
        return remote(
            gtx.at[j, pl.ds(PART, PART)], r1.at[1, j, k], s1_send.at[1, j], s1_recv.at[1, j, k], dev(x, ym, c)
        )

    @pl.loop(0, HALF)
    def _(j):
        real, xm, ym = owner(j)

        @pl.when(real)
        def _():
            m = HALF * c + j
            remote(gx.at[j], gx.at[j], x_send.at[j], x_recv.at[j], partner).wait_recv()
            remote(mx.at[j], mx.at[j], mx_send.at[j], mx_recv.at[j], partner).wait_recv()
            xx[j, 0] = prepare(gbuf[m], mbuf[m])
            xx[j, 1] = prepare(gx[j], mx[j])
            value = jnp.concatenate([xx[j, 0], xx[j, 1]], axis=1)
            top = dot_nt(value[:128], value[:256])
            mid = dot_nt(value[128:256], value[128:256])
            low = dot_nt(value[256:288], value)
            pieces = pack(top[:, :128], top[:, 128:], mid, low)
            own_scale = scale(x, y)
            for at, piece in pieces:
                gloc[j, at : at + piece.shape[0]] = piece
                gtx[j, at : at + piece.shape[0]] = (piece * own_scale).astype(BF16)

            @pl.when(xm != x)
            def _():
                s1_x(j, xm).start()

            @pl.when(ym != y)
            def _():
                s1_y(j, ym).start()

    @pl.loop(0, MATS)
    def _(i):
        nmbuf[i] = DECAY * mbuf[i] + gbuf[i].astype(F32) * clip
        store_nm(i).start()

    def s2_x(j, ym):
        k = slot(y, ym)
        return remote(s2.at[0, j], r2.at[0, k], s2_send.at[0, j], s2_recv.at[0, k], dev(x, ym, c))

    def s2_y(j, xm):
        k = slot(x, xm)
        return remote(s2.at[1, j], r2.at[1, k], s2_send.at[1, j], s2_recv.at[1, k], dev(xm, y, c))

    def wait_r1(half, j, k):
        remote(r1.at[half, j, k], r1.at[half, j, k], s1_send.at[half, j], s1_recv.at[half, j, k], partner).wait_recv()

    def wait_r2(half, k):
        remote(r2.at[half, k], r2.at[half, k], s2_send.at[half, 0], s2_recv.at[half, k], partner).wait_recv()

    @pl.loop(0, HALF)
    def _(j):
        real, xm, ym = owner(j)

        def reduce(half, near, far, start):
            @pl.when(real & near)
            def _():
                for k in range(3):
                    wait_r1(half, j, k)
                total = gloc[j, PART * half : PART * half + PART]
                for k in range(3):
                    from_x = (x + k + 1) % 4 if half == 0 else x
                    from_y = y if half == 0 else (y + k + 1) % 4
                    total = total + r1[half, j, k].astype(F32) * (1.0 / scale(from_x, from_y))
                gloc[j, PART * half : PART * half + PART] = total

                @pl.when(far)
                def _():
                    s2[half, j] = (total * scale(x, y)).astype(BF16)
                    start()

        reduce(0, xm == x, ym != y, lambda: s2_x(j, ym).start())
        reduce(1, ym == y, xm != x, lambda: s2_y(j, xm).start())

    def q1_copy(j, half, k, o):
        target = dev(x, (y + o) % 4, c) if half == 0 else dev((x + o) % 4, y, c)
        return remote(
            qbuf.at[j, half, k], qbuf.at[j, half, k], q1_send.at[half, k, o - 1], q_recv.at[j, half, k], target
        )

    def q2_copy(j, half, k, o):
        target = dev((x + o) % 4, y, c) if half == 0 else dev(x, (y + o) % 4, c)
        return remote(
            qbuf.at[j, half, k], qbuf.at[j, half, k], q2_send.at[j, half, k, o - 1], q_recv.at[j, half, k], target
        )

    @pl.loop(0, HALF)
    def _(j):
        real, xm, ym = owner(j)

        @pl.when(real & (xm == x) & (ym == y))
        def _():
            for half in range(2):
                for k in range(3):
                    wait_r2(half, k)
                total = gloc[j, PART * half : PART * half + PART]
                for k in range(3):
                    from_x = x if half == 0 else (x + k + 1) % 4
                    from_y = (y + k + 1) % 4 if half == 0 else y
                    total = total + r2[half, k].astype(F32) * (1.0 / scale(from_x, from_y))
                gloc[j, PART * half : PART * half + PART] = total
            unpack(
                gf,
                gloc[j, 0:128],
                gloc[j, 128:256],
                gloc[j, 256:288],
                gloc[j, 288:320],
                gloc[j, 320:352],
            )
            row = lax.broadcasted_iota(jnp.int32, (ROWS, ROWS), 0)
            col = lax.broadcasted_iota(jnp.int32, (ROWS, ROWS), 1)
            diag = row == col
            raw = gf[...]
            norm = jnp.sqrt(jnp.sum(jnp.where(diag, raw, 0.0), keepdims=True)) + 1e-07
            inverse = 1.0 / norm
            gram = raw * (inverse * inverse)
            gram_s = split(gram)
            poly = TWO * gram + THREE * product(gram_s, gram_s) + jnp.where(diag, ONE, 0.0)
            poly_s = split(poly)
            left_s = split(product(poly_s, gram_s))
            gram = product(left_s, poly_s)
            gram_s = split(gram)
            last = TWO * gram + THREE * product(gram_s, gram_s) + jnp.where(diag, ONE, 0.0)
            gf[...] = product(split(last), poly_s) * (WIDTH_SCALE * inverse)

            pieces = pack(gf[0:128, 0:128], gf[0:128, 128:256], gf[128:256, 128:256], gf[256:288, :])
            for at, piece in pieces:
                both = split(piece)
                size = piece.shape[0]
                for half in range(2):
                    lo = max(at, PART * half)
                    hi = min(at + size, PART * half + PART)
                    if lo < hi:
                        for k in range(2):
                            qbuf[j, half, k, lo - PART * half : hi - PART * half] = both[k][lo - at : hi - at]
            for k in range(2):
                for half in range(2):
                    for o in (2, 1, 3):
                        q1_copy(j, half, k, o).start()

    def wait_q(j, half, k):
        remote(
            qbuf.at[j, half, k], qbuf.at[j, half, k], q1_send.at[half, k, 0], q_recv.at[j, half, k], partner
        ).wait_recv()

    for k in range(2):

        @pl.loop(0, HALF)
        def _(j):
            real, xm, ym = owner(j)

            def forward(half, near, far):
                @pl.when(real & near)
                def _():
                    @pl.when(far)
                    def _():
                        wait_q(j, half, k)

                    for o in (2, 1, 3):
                        q2_copy(j, half, k, o).start()

            forward(0, xm == x, ym != y)
            forward(1, ym == y, xm != x)

    @pl.loop(0, MATS)
    def _(i):
        store_nm(i).wait()

    @pl.loop(1, 16)
    def _(o):
        z_copy(o).wait_send()
        p_copy(o).wait_send()

    core_copy().wait_send()

    @pl.loop(0, HALF)
    def _(j):
        real, xm, ym = owner(j)

        @pl.when(HALF * (1 - c) + j < MATS)
        def _():
            gx_copy(j).wait_send()
            mx_copy(j).wait_send()

        @pl.when(real)
        def _():
            @pl.when(xm != x)
            def _():
                s1_x(j, xm).wait_send()

            @pl.when(ym != y)
            def _():
                s1_y(j, ym).wait_send()

            @pl.when((xm == x) & (ym != y))
            def _():
                s2_x(j, ym).wait_send()

            @pl.when((ym == y) & (xm != x))
            def _():
                s2_y(j, xm).wait_send()

    def o_copy(j):
        m = HALF * c + j
        return remote(obuf.at[j, 1], o_hbm.at[m], o_send.at[j], o_recv.at[j], partner)

    def o_local(j):
        m = HALF * c + j
        return pltpu.make_async_copy(obuf.at[j, 0], o_hbm.at[m], ol_sem.at[j])

    @pl.loop(0, HALF)
    def _(j):
        real, xm, ym = owner(j)

        @pl.when(real)
        def _():
            @pl.when(xm != x)
            def _():
                wait_q(j, 0, 0)
                wait_q(j, 0, 1)

            @pl.when(ym != y)
            def _():
                wait_q(j, 1, 0)
                wait_q(j, 1, 1)

            first = qbuf[j, 0, 0].astype(F32) + qbuf[j, 0, 1].astype(F32)
            second = qbuf[j, 1, 0].astype(F32) + qbuf[j, 1, 1].astype(F32)
            cross = jnp.concatenate([first[128:176], second[0:80]], axis=0)
            unpack(gf, first[0:128], cross, second[80:112], second[112:144], second[144:176])
            full = split(gf[...])
            value = jnp.concatenate([xx[j, 0], xx[j, 1]], axis=1)
            result = (dot(full[0], value) + dot(full[1], value)).astype(BF16)
            obuf[j, 0] = result[:, :128]
            obuf[j, 1] = result[:, 128:]
            o_local(j).start()
            o_copy(j).start()

    @pl.loop(0, HALF)
    def _(j):
        real, xm, ym = owner(j)

        @pl.when(real & (xm == x) & (ym == y))
        def _():
            for k in range(2):
                for half in range(2):
                    for o in range(1, 4):
                        q1_copy(j, half, k, o).wait_send()

        @pl.when(real & (xm == x))
        def _():
            for k in range(2):
                for o in range(1, 4):
                    q2_copy(j, 0, k, o).wait_send()

        @pl.when(real & (ym == y))
        def _():
            for k in range(2):
                for o in range(1, 4):
                    q2_copy(j, 1, k, o).wait_send()

    @pl.loop(0, HALF)
    def _(j):
        @pl.when(HALF * (1 - c) + j < MATS)
        def _():
            remote(obuf.at[j, 1], obuf.at[j, 1], o_send.at[j], o_recv.at[j], partner).wait_recv()

        @pl.when(HALF * c + j < MATS)
        def _():
            o_local(j).wait()
            o_copy(j).wait_send()


def per_device(gradients, momentum):
    dma = pltpu.SemaphoreType.DMA
    vmem = pltpu.VMEM
    any_spec = pl.BlockSpec(memory_space=pl.ANY)
    return pl.pallas_call(
        kernel,
        out_shape=(
            jax.ShapeDtypeStruct((MATS, ROWS, COLS), F32),
            jax.ShapeDtypeStruct((MATS, ROWS, COLS), BF16),
        ),
        in_specs=[pl.BlockSpec(memory_space=pltpu.HBM)] * 2,
        out_specs=(any_spec, any_spec),
        scratch_shapes=[
            vmem((MATS, ROWS, COLS), BF16),
            vmem((MATS, ROWS, COLS), F32),
            vmem((MATS, ROWS, COLS), F32),
            vmem((3, 8, COLS), F32),
            vmem((15, 8, COLS), F32),
            vmem((16, 8, COLS), F32),
            vmem((HALF, ROWS, COLS), BF16),
            vmem((HALF, ROWS, COLS), F32),
            vmem((HALF, 2, ROWS, COLS), BF16),
            vmem((HALF, PACK, COLS), F32),
            vmem((HALF, PACK, COLS), BF16),
            vmem((2, HALF, 3, PART, COLS), BF16),
            vmem((2, HALF, PART, COLS), BF16),
            vmem((2, 3, PART, COLS), BF16),
            vmem((ROWS, ROWS), F32),
            vmem((HALF, 2, 2, PART, COLS), BF16),
            vmem((HALF, 2, ROWS, COLS), BF16),
            dma((MATS,)),
            dma((MATS,)),
            dma((MATS,)),
            dma((15,)),
            dma((15,)),
            dma((16,)),
            dma((16,)),
            dma((HALF,)),
            dma((HALF,)),
            dma((HALF,)),
            dma((HALF,)),
            dma((2, HALF)),
            dma((2, HALF, 3)),
            dma((2, HALF)),
            dma((2, 3)),
            dma((2, 2, 3)),
            dma((HALF, 2, 2, 3)),
            dma((HALF, 2, 2)),
            dma((HALF,)),
            dma((HALF,)),
            dma((HALF,)),
            pltpu.SemaphoreType.REGULAR((2,)),
        ],
        compiler_params=pltpu.CompilerParams(
            collective_id=0, has_side_effects=True, vmem_limit_bytes=40 * 1024 * 1024
        ),
        cost_estimate=pl.CostEstimate(flops=1500000000, bytes_accessed=5000000, transcendentals=0),
        name="muon",
    )(
        pltpu.with_memory_space_constraint(gradients, pltpu.HBM),
        pltpu.with_memory_space_constraint(momentum, pltpu.HBM),
    )


def solution(mesh):
    placed = (P("section", None, "dp"), P("section", None, "dp"))
    return jax.shard_map(
        per_device, mesh=mesh, in_specs=placed, out_specs=placed, check_vma=False
    )
```

```python
import jax
import jax.numpy as jnp
from jax import lax
from jax.experimental import pallas as pl
from jax.experimental.pallas import tpu as pltpu
from jax.sharding import PartitionSpec as P

MATS = 11
ROWS = 288
COLS = 128
HALF = 6
PACK = 352
PART = 176
ENTRIES = 176 * 288 * 4096
WIDTH_SCALE = 64.0

DECAY = 0.95
ONE = 3.4445
TWO = -4.775
THREE = 2.0315

F32 = jnp.float32
BF16 = jnp.bfloat16
MESH = pl.DeviceIdType.MESH


def dot(a, b):
    return jnp.dot(a, b, preferred_element_type=F32)


def dot_nt(a, b):
    return lax.dot_general(a, b, (((1,), (1,)), ((), ())), preferred_element_type=F32)


def split(a):
    high = a.astype(BF16)
    return high, (a - high.astype(F32)).astype(BF16)


def product(a, b):
    wide, tail = slice(0, 256), slice(256, 288)
    left = jnp.concatenate(
        [a[0][:, wide], a[0][:, wide], a[1][:, wide], a[0][:, tail], a[0][:, tail], a[1][:, tail]], axis=1
    )
    right = jnp.concatenate([b[0][wide], b[1][wide], b[0][wide], b[0][tail], b[1][tail], b[0][tail]], axis=0)
    main = dot(left, right[:, wide])
    corner = dot(left[tail], right[:, tail])
    side = jnp.concatenate([main[tail].T, corner], axis=0)
    return jnp.concatenate([main, side], axis=1)


def triangle():
    row = lax.broadcasted_iota(jnp.int32, (128, 128), 0)
    col = lax.broadcasted_iota(jnp.int32, (128, 128), 1)
    return row, col


def pack(first, cross, second, low):
    row, col = triangle()
    middle = jnp.sum(jnp.where(row == col, second, 0.0), axis=0, keepdims=True)
    rest = jnp.concatenate([middle[:, 96:128], jnp.zeros((1, 64), F32)], axis=1)
    beside = jnp.concatenate(
        [jnp.broadcast_to(middle[:, 0:96], (16, 96)), jnp.broadcast_to(rest, (16, 96))], axis=0
    )
    corner = jnp.concatenate([low[:, 256:288], beside], axis=1)
    return (
        (0, jnp.where(col >= row, first, second)),
        (128, cross),
        (256, low[:, :128]),
        (288, low[:, 128:256]),
        (320, corner),
    )


def unpack(full, both, cross, low0, low1, corner):
    row, col = triangle()
    middle = jnp.concatenate([corner[0:1, 32:128], corner[16:17, 32:64]], axis=1)
    turned = both.T
    low = jnp.concatenate([low0, low1], axis=1)
    full[0:128, 0:128] = jnp.where(col >= row, both, turned)
    full[0:128, 128:256] = cross
    full[128:256, 0:128] = cross.T
    full[128:256, 128:256] = jnp.where(
        row == col, jnp.broadcast_to(middle, (128, 128)), jnp.where(row > col, both, turned)
    )
    full[256:288, 0:256] = low
    full[0:256, 256:288] = low.T
    full[256:288, 256:288] = corner[:, :32]


def kernel(
    g_hbm,
    m_hbm,
    nm_out,
    o_hbm,
    gbuf,
    mbuf,
    nmbuf,
    acc,
    accz,
    accp,
    gx,
    mx,
    xx,
    gloc,
    gtx,
    r1,
    s2,
    r2,
    gf,
    qbuf,
    obuf,
    g_sem,
    m_sem,
    nm_sem,
    z_send,
    z_recv,
    p_send,
    p_recv,
    x_send,
    x_recv,
    mx_send,
    mx_recv,
    s1_send,
    s1_recv,
    s2_send,
    s2_recv,
    q1_send,
    q2_send,
    q_recv,
    o_send,
    o_recv,
    ol_sem,
    relay,
):
    z = lax.axis_index("section")
    d = lax.axis_index("dp")
    x = d // 8
    y = (d // 2) % 4
    c = d % 2

    def dev(px, py, pc):
        return (z, (px * 4 + py) * 2 + pc)

    partner = dev(x, y, 1 - c)

    def remote(src, dst, send, recv, target):
        return pltpu.make_async_remote_copy(
            src_ref=src, dst_ref=dst, send_sem=send, recv_sem=recv, device_id=target, device_id_type=MESH
        )

    def load_g(i):
        return pltpu.make_async_copy(g_hbm.at[i], gbuf.at[i], g_sem.at[i])

    def store_nm(i):
        return pltpu.make_async_copy(nmbuf.at[i], nm_out.at[i], nm_sem.at[i])

    def load_m(i):
        return pltpu.make_async_copy(m_hbm.at[i], mbuf.at[i], m_sem.at[i])

    barrier = pltpu.get_barrier_semaphore()

    def greet(target):
        pl.semaphore_signal(barrier, inc=1, device_id=target, device_id_type=MESH)

    @pl.loop(1, 5)
    def _(o):
        greet((lax.rem(z + o, 16), d))
        greet((lax.rem(z + 16 - o, 16), d))

    @pl.loop(1, 16)
    def _(o):
        greet(dev((x + o // 4) % 4, (y + o) % 4, c))

    greet(partner)

    @pl.loop(0, MATS)
    def _(i):
        load_g(i).start()

    def squares(i, total):
        load_g(i).wait()
        value = gbuf[i].astype(F32)
        return total + jnp.sum((value * value).reshape(ROWS // 8, 8, COLS), axis=0)

    total = lax.fori_loop(0, MATS, squares, jnp.zeros((8, COLS), F32))
    acc[0, 0:1] = jnp.sum(total, axis=0, keepdims=True)

    @pl.loop(0, MATS)
    def _(i):
        load_m(i).start()

    pl.semaphore_wait(barrier, 24)

    pl.semaphore_signal(relay.at[0], inc=1, device_id=(lax.rem(z + 4, 16), d), device_id_type=MESH)
    pl.semaphore_signal(relay.at[1], inc=1, device_id=(lax.rem(z + 12, 16), d), device_id_type=MESH)

    def core_copy():
        return remote(
            acc.at[0, pl.ds(0, 1)], accp.at[15, pl.ds(0, 1)], p_send.at[15], p_recv.at[15], partner
        )

    core_copy().start()
    core_copy().wait_recv()
    acc[1, 0:1] = acc[0, 0:1] + accp[15, 0:1]

    def p_copy(o):
        return remote(
            acc.at[1, pl.ds(0, 1)],
            accp.at[o - 1, pl.ds(0, 1)],
            p_send.at[o - 1],
            p_recv.at[o - 1],
            dev((x + o // 4) % 4, (y + o) % 4, c),
        )

    @pl.loop(1, 16)
    def _(o):
        p_copy(o).start()

    def gx_copy(j):
        return remote(gbuf.at[HALF * (1 - c) + j], gx.at[j], x_send.at[j], x_recv.at[j], partner)

    def mx_copy(j):
        return remote(mbuf.at[HALF * (1 - c) + j], mx.at[j], mx_send.at[j], mx_recv.at[j], partner)

    @pl.loop(0, MATS)
    def _(i):
        load_m(i).wait()

    @pl.loop(0, HALF)
    def _(j):
        @pl.when(HALF * (1 - c) + j < MATS)
        def _():
            gx_copy(j).start()
            mx_copy(j).start()

    pl.semaphore_wait(relay.at[0], 1)
    pl.semaphore_wait(relay.at[1], 1)

    @pl.loop(1, 16)
    def _(o):
        p_copy(o).wait_recv()

    acc[2, 0:1] = acc[1, 0:1] + jnp.sum(accp[0:15, 0:1, :], axis=0)

    def z_copy(o):
        return remote(
            acc.at[2, pl.ds(0, 1)],
            accz.at[o - 1, pl.ds(0, 1)],
            z_send.at[o - 1],
            z_recv.at[o - 1],
            (lax.rem(z + o, 16), d),
        )

    @pl.loop(1, 16)
    def _(o):
        z_copy(o).start()

    @pl.loop(1, 16)
    def _(o):
        z_copy(o).wait_recv()

    mean = jnp.sum(acc[2, 0:1] + jnp.sum(accz[:, 0:1, :], axis=0), keepdims=True) / ENTRIES + 1e-06
    root = lax.rsqrt(mean)
    root = root * (1.5 - 0.5 * mean * root * root)
    clip = jnp.minimum(1.0, root)

    def prepare(gradient, moment):
        scaled = gradient.astype(F32) * clip
        return (scaled + DECAY * (DECAY * moment + scaled)).astype(BF16)

    def owner(j):
        m = HALF * c + j
        return m < MATS, m % 4, (m // 4 + m % 4) % 4

    def slot(own, at):
        return jnp.maximum((own - at + 4) % 4 - 1, 0)

    def scale(px, py):
        return jnp.broadcast_to((16 + px * 4 + py).astype(F32) * 0.0625, (1, COLS))

    def s1_x(j, xm):
        k = slot(x, xm)
        return remote(
            gtx.at[j, pl.ds(0, PART)], r1.at[0, j, k], s1_send.at[0, j], s1_recv.at[0, j, k], dev(xm, y, c)
        )

    def s1_y(j, ym):
        k = slot(y, ym)
        return remote(
            gtx.at[j, pl.ds(PART, PART)], r1.at[1, j, k], s1_send.at[1, j], s1_recv.at[1, j, k], dev(x, ym, c)
        )

    @pl.loop(0, HALF)
    def _(j):
        real, xm, ym = owner(j)

        @pl.when(real)
        def _():
            m = HALF * c + j
            remote(gx.at[j], gx.at[j], x_send.at[j], x_recv.at[j], partner).wait_recv()
            remote(mx.at[j], mx.at[j], mx_send.at[j], mx_recv.at[j], partner).wait_recv()
            xx[j, 0] = prepare(gbuf[m], mbuf[m])
            xx[j, 1] = prepare(gx[j], mx[j])
            value = jnp.concatenate([xx[j, 0], xx[j, 1]], axis=1)
            top = dot_nt(value[:128], value[:256])
            mid = dot_nt(value[128:256], value[128:256])
            low = dot_nt(value[256:288], value)
            pieces = pack(top[:, :128], top[:, 128:], mid, low)
            own_scale = scale(x, y)
            for at, piece in pieces:
                gloc[j, at : at + piece.shape[0]] = piece
                gtx[j, at : at + piece.shape[0]] = (piece * own_scale).astype(BF16)

            @pl.when(xm != x)
            def _():
                s1_x(j, xm).start()

            @pl.when(ym != y)
            def _():
                s1_y(j, ym).start()

    def s2_x(j, ym):
        k = slot(y, ym)
        return remote(s2.at[0, j], r2.at[0, k], s2_send.at[0, j], s2_recv.at[0, k], dev(x, ym, c))

    def s2_y(j, xm):
        k = slot(x, xm)
        return remote(s2.at[1, j], r2.at[1, k], s2_send.at[1, j], s2_recv.at[1, k], dev(xm, y, c))

    def wait_r1(half, j, k):
        remote(r1.at[half, j, k], r1.at[half, j, k], s1_send.at[half, j], s1_recv.at[half, j, k], partner).wait_recv()

    def wait_r2(half, k):
        remote(r2.at[half, k], r2.at[half, k], s2_send.at[half, 0], s2_recv.at[half, k], partner).wait_recv()

    @pl.loop(0, HALF)
    def _(j):
        real, xm, ym = owner(j)

        def reduce(half, near, far, start):
            @pl.when(real & near)
            def _():
                for k in range(3):
                    wait_r1(half, j, k)
                total = gloc[j, PART * half : PART * half + PART]
                for k in range(3):
                    from_x = (x + k + 1) % 4 if half == 0 else x
                    from_y = y if half == 0 else (y + k + 1) % 4
                    total = total + r1[half, j, k].astype(F32) * (1.0 / scale(from_x, from_y))
                gloc[j, PART * half : PART * half + PART] = total

                @pl.when(far)
                def _():
                    s2[half, j] = (total * scale(x, y)).astype(BF16)
                    start()

        reduce(0, xm == x, ym != y, lambda: s2_x(j, ym).start())
        reduce(1, ym == y, xm != x, lambda: s2_y(j, xm).start())

    def q1_copy(j, half, k, o):
        target = dev(x, (y + o) % 4, c) if half == 0 else dev((x + o) % 4, y, c)
        return remote(
            qbuf.at[j, half, k], qbuf.at[j, half, k], q1_send.at[half, k, o - 1], q_recv.at[j, half, k], target
        )

    def q2_copy(j, half, k, o):
        target = dev((x + o) % 4, y, c) if half == 0 else dev(x, (y + o) % 4, c)
        return remote(
            qbuf.at[j, half, k], qbuf.at[j, half, k], q2_send.at[j, half, k, o - 1], q_recv.at[j, half, k], target
        )

    @pl.loop(0, HALF)
    def _(j):
        real, xm, ym = owner(j)

        @pl.when(real & (xm == x) & (ym == y))
        def _():
            for half in range(2):
                for k in range(3):
                    wait_r2(half, k)
                total = gloc[j, PART * half : PART * half + PART]
                for k in range(3):
                    from_x = x if half == 0 else (x + k + 1) % 4
                    from_y = (y + k + 1) % 4 if half == 0 else y
                    total = total + r2[half, k].astype(F32) * (1.0 / scale(from_x, from_y))
                gloc[j, PART * half : PART * half + PART] = total
            unpack(
                gf,
                gloc[j, 0:128],
                gloc[j, 128:256],
                gloc[j, 256:288],
                gloc[j, 288:320],
                gloc[j, 320:352],
            )
            row = lax.broadcasted_iota(jnp.int32, (ROWS, ROWS), 0)
            col = lax.broadcasted_iota(jnp.int32, (ROWS, ROWS), 1)
            diag = row == col
            raw = gf[...]
            norm = jnp.sqrt(jnp.sum(jnp.where(diag, raw, 0.0), keepdims=True)) + 1e-07
            inverse = 1.0 / norm
            gram = raw * (inverse * inverse)
            gram_s = split(gram)
            poly = TWO * gram + THREE * product(gram_s, gram_s) + jnp.where(diag, ONE, 0.0)
            poly_s = split(poly)
            left_s = split(product(poly_s, gram_s))
            gram = product(left_s, poly_s)
            gram_s = split(gram)
            last = TWO * gram + THREE * product(gram_s, gram_s) + jnp.where(diag, ONE, 0.0)
            gf[...] = product(split(last), poly_s) * (WIDTH_SCALE * inverse)

            pieces = pack(gf[0:128, 0:128], gf[0:128, 128:256], gf[128:256, 128:256], gf[256:288, :])
            for at, piece in pieces:
                both = split(piece)
                size = piece.shape[0]
                for half in range(2):
                    lo = max(at, PART * half)
                    hi = min(at + size, PART * half + PART)
                    if lo < hi:
                        for k in range(2):
                            qbuf[j, half, k, lo - PART * half : hi - PART * half] = both[k][lo - at : hi - at]
            for k in range(2):
                for half in range(2):
                    for o in (2, 1, 3):
                        q1_copy(j, half, k, o).start()

    def wait_q(j, half, k):
        remote(
            qbuf.at[j, half, k], qbuf.at[j, half, k], q1_send.at[half, k, 0], q_recv.at[j, half, k], partner
        ).wait_recv()

    for k in range(2):

        @pl.loop(0, HALF)
        def _(j):
            real, xm, ym = owner(j)

            def forward(half, near, far):
                @pl.when(real & near)
                def _():
                    @pl.when(far)
                    def _():
                        wait_q(j, half, k)

                    for o in (2, 1, 3):
                        q2_copy(j, half, k, o).start()

            forward(0, xm == x, ym != y)
            forward(1, ym == y, xm != x)

    @pl.loop(0, MATS)
    def _(i):
        nmbuf[i] = DECAY * mbuf[i] + gbuf[i].astype(F32) * clip
        store_nm(i).start()

    @pl.loop(0, MATS)
    def _(i):
        store_nm(i).wait()

    @pl.loop(1, 16)
    def _(o):
        z_copy(o).wait_send()
        p_copy(o).wait_send()

    core_copy().wait_send()

    @pl.loop(0, HALF)
    def _(j):
        real, xm, ym = owner(j)

        @pl.when(HALF * (1 - c) + j < MATS)
        def _():
            gx_copy(j).wait_send()
            mx_copy(j).wait_send()

        @pl.when(real)
        def _():
            @pl.when(xm != x)
            def _():
                s1_x(j, xm).wait_send()

            @pl.when(ym != y)
            def _():
                s1_y(j, ym).wait_send()

            @pl.when((xm == x) & (ym != y))
            def _():
                s2_x(j, ym).wait_send()

            @pl.when((ym == y) & (xm != x))
            def _():
                s2_y(j, xm).wait_send()

    def o_copy(j):
        m = HALF * c + j
        return remote(obuf.at[j, 1], o_hbm.at[m], o_send.at[j], o_recv.at[j], partner)

    def o_local(j):
        m = HALF * c + j
        return pltpu.make_async_copy(obuf.at[j, 0], o_hbm.at[m], ol_sem.at[j])

    @pl.loop(0, HALF)
    def _(j):
        real, xm, ym = owner(j)

        @pl.when(real)
        def _():
            @pl.when(xm != x)
            def _():
                wait_q(j, 0, 0)
                wait_q(j, 0, 1)

            @pl.when(ym != y)
            def _():
                wait_q(j, 1, 0)
                wait_q(j, 1, 1)

            first = qbuf[j, 0, 0].astype(F32) + qbuf[j, 0, 1].astype(F32)
            second = qbuf[j, 1, 0].astype(F32) + qbuf[j, 1, 1].astype(F32)
            cross = jnp.concatenate([first[128:176], second[0:80]], axis=0)
            unpack(gf, first[0:128], cross, second[80:112], second[112:144], second[144:176])
            full = split(gf[...])
            value = jnp.concatenate([xx[j, 0], xx[j, 1]], axis=1)
            result = (dot(full[0], value) + dot(full[1], value)).astype(BF16)
            obuf[j, 0] = result[:, :128]
            obuf[j, 1] = result[:, 128:]
            o_copy(j).start()
            o_local(j).start()

    @pl.loop(0, HALF)
    def _(j):
        real, xm, ym = owner(j)

        @pl.when(real & (xm == x) & (ym == y))
        def _():
            for k in range(2):
                for half in range(2):
                    for o in range(1, 4):
                        q1_copy(j, half, k, o).wait_send()

        @pl.when(real & (xm == x))
        def _():
            for k in range(2):
                for o in range(1, 4):
                    q2_copy(j, 0, k, o).wait_send()

        @pl.when(real & (ym == y))
        def _():
            for k in range(2):
                for o in range(1, 4):
                    q2_copy(j, 1, k, o).wait_send()

    @pl.loop(0, HALF)
    def _(j):
        @pl.when(HALF * (1 - c) + j < MATS)
        def _():
            remote(obuf.at[j, 1], obuf.at[j, 1], o_send.at[j], o_recv.at[j], partner).wait_recv()

        @pl.when(HALF * c + j < MATS)
        def _():
            o_local(j).wait()
            o_copy(j).wait_send()


def per_device(gradients, momentum):
    dma = pltpu.SemaphoreType.DMA
    vmem = pltpu.VMEM
    any_spec = pl.BlockSpec(memory_space=pl.ANY)
    return pl.pallas_call(
        kernel,
        out_shape=(
            jax.ShapeDtypeStruct((MATS, ROWS, COLS), F32),
            jax.ShapeDtypeStruct((MATS, ROWS, COLS), BF16),
        ),
        in_specs=[pl.BlockSpec(memory_space=pltpu.HBM)] * 2,
        out_specs=(any_spec, any_spec),
        scratch_shapes=[
            vmem((MATS, ROWS, COLS), BF16),
            vmem((MATS, ROWS, COLS), F32),
            vmem((MATS, ROWS, COLS), F32),
            vmem((3, 8, COLS), F32),
            vmem((15, 8, COLS), F32),
            vmem((16, 8, COLS), F32),
            vmem((HALF, ROWS, COLS), BF16),
            vmem((HALF, ROWS, COLS), F32),
            vmem((HALF, 2, ROWS, COLS), BF16),
            vmem((HALF, PACK, COLS), F32),
            vmem((HALF, PACK, COLS), BF16),
            vmem((2, HALF, 3, PART, COLS), BF16),
            vmem((2, HALF, PART, COLS), BF16),
            vmem((2, 3, PART, COLS), BF16),
            vmem((ROWS, ROWS), F32),
            vmem((HALF, 2, 2, PART, COLS), BF16),
            vmem((HALF, 2, ROWS, COLS), BF16),
            dma((MATS,)),
            dma((MATS,)),
            dma((MATS,)),
            dma((15,)),
            dma((15,)),
            dma((16,)),
            dma((16,)),
            dma((HALF,)),
            dma((HALF,)),
            dma((HALF,)),
            dma((HALF,)),
            dma((2, HALF)),
            dma((2, HALF, 3)),
            dma((2, HALF)),
            dma((2, 3)),
            dma((2, 2, 3)),
            dma((HALF, 2, 2, 3)),
            dma((HALF, 2, 2)),
            dma((HALF,)),
            dma((HALF,)),
            dma((HALF,)),
            pltpu.SemaphoreType.REGULAR((2,)),
        ],
        compiler_params=pltpu.CompilerParams(
            collective_id=0, has_side_effects=True, vmem_limit_bytes=40 * 1024 * 1024
        ),
        cost_estimate=pl.CostEstimate(flops=1500000000, bytes_accessed=5000000, transcendentals=0),
        name="muon",
    )(
        pltpu.with_memory_space_constraint(gradients, pltpu.HBM),
        pltpu.with_memory_space_constraint(momentum, pltpu.HBM),
    )


def solution(mesh):
    placed = (P("section", None, "dp"), P("section", None, "dp"))
    return jax.shard_map(
        per_device, mesh=mesh, in_specs=placed, out_specs=placed, check_vma=False
    )
```

```python
import jax
import jax.numpy as jnp
from jax import lax
from jax.experimental import pallas as pl
from jax.experimental.pallas import tpu as pltpu
from jax.sharding import PartitionSpec as P

MATS = 11
ROWS = 288
COLS = 128
HALF = 6
PACK = 352
PART = 176
ENTRIES = 176 * 288 * 4096
WIDTH_SCALE = 64.0

DECAY = 0.95
ONE = 3.4445
TWO = -4.775
THREE = 2.0315

F32 = jnp.float32
BF16 = jnp.bfloat16
MESH = pl.DeviceIdType.MESH


def dot(a, b):
    return jnp.dot(a, b, preferred_element_type=F32)


def dot_nt(a, b):
    return lax.dot_general(a, b, (((1,), (1,)), ((), ())), preferred_element_type=F32)


def split(a):
    high = a.astype(BF16)
    return high, (a - high.astype(F32)).astype(BF16)


def product(a, b):
    wide, tail = slice(0, 256), slice(256, 288)
    left = jnp.concatenate(
        [a[0][:, wide], a[0][:, wide], a[1][:, wide], a[0][:, tail], a[0][:, tail], a[1][:, tail]], axis=1
    )
    right = jnp.concatenate([b[0][wide], b[1][wide], b[0][wide], b[0][tail], b[1][tail], b[0][tail]], axis=0)
    main = dot(left, right[:, wide])
    corner = dot(left[tail], right[:, tail])
    side = jnp.concatenate([main[tail].T, corner], axis=0)
    return jnp.concatenate([main, side], axis=1)


def triangle():
    row = lax.broadcasted_iota(jnp.int32, (128, 128), 0)
    col = lax.broadcasted_iota(jnp.int32, (128, 128), 1)
    return row, col


def pack(first, cross, second, low):
    row, col = triangle()
    middle = jnp.sum(jnp.where(row == col, second, 0.0), axis=0, keepdims=True)
    rest = jnp.concatenate([middle[:, 96:128], jnp.zeros((1, 64), F32)], axis=1)
    beside = jnp.concatenate(
        [jnp.broadcast_to(middle[:, 0:96], (16, 96)), jnp.broadcast_to(rest, (16, 96))], axis=0
    )
    corner = jnp.concatenate([low[:, 256:288], beside], axis=1)
    return (
        (0, jnp.where(col >= row, first, second)),
        (128, cross),
        (256, low[:, :128]),
        (288, low[:, 128:256]),
        (320, corner),
    )


def unpack(full, both, cross, low0, low1, corner):
    row, col = triangle()
    middle = jnp.concatenate([corner[0:1, 32:128], corner[16:17, 32:64]], axis=1)
    turned = both.T
    low = jnp.concatenate([low0, low1], axis=1)
    full[0:128, 0:128] = jnp.where(col >= row, both, turned)
    full[0:128, 128:256] = cross
    full[128:256, 0:128] = cross.T
    full[128:256, 128:256] = jnp.where(
        row == col, jnp.broadcast_to(middle, (128, 128)), jnp.where(row > col, both, turned)
    )
    full[256:288, 0:256] = low
    full[0:256, 256:288] = low.T
    full[256:288, 256:288] = corner[:, :32]


def kernel(
    g_hbm,
    m_hbm,
    nm_out,
    o_hbm,
    gbuf,
    mbuf,
    nmbuf,
    acc,
    accz,
    accp,
    gx,
    mx,
    xx,
    gloc,
    gtx,
    r1,
    s2,
    r2,
    gf,
    qbuf,
    obuf,
    g_sem,
    m_sem,
    nm_sem,
    z_send,
    z_recv,
    p_send,
    p_recv,
    x_send,
    x_recv,
    mx_send,
    mx_recv,
    s1_send,
    s1_recv,
    s2_send,
    s2_recv,
    q1_send,
    q2_send,
    q_recv,
    o_send,
    o_recv,
    ol_sem,
    relay,
):
    z = lax.axis_index("section")
    d = lax.axis_index("dp")
    x = d // 8
    y = (d // 2) % 4
    c = d % 2

    def dev(px, py, pc):
        return (z, (px * 4 + py) * 2 + pc)

    partner = dev(x, y, 1 - c)

    def remote(src, dst, send, recv, target):
        return pltpu.make_async_remote_copy(
            src_ref=src, dst_ref=dst, send_sem=send, recv_sem=recv, device_id=target, device_id_type=MESH
        )

    def load_g(i):
        return pltpu.make_async_copy(g_hbm.at[i], gbuf.at[i], g_sem.at[i])

    def store_nm(i):
        return pltpu.make_async_copy(nmbuf.at[i], nm_out.at[i], nm_sem.at[i])

    def load_m(i):
        return pltpu.make_async_copy(m_hbm.at[i], mbuf.at[i], m_sem.at[i])

    barrier = pltpu.get_barrier_semaphore()

    def greet(target):
        pl.semaphore_signal(barrier, inc=1, device_id=target, device_id_type=MESH)

    @pl.loop(1, 5)
    def _(o):
        greet((lax.rem(z + o, 16), d))
        greet((lax.rem(z + 16 - o, 16), d))

    @pl.loop(1, 16)
    def _(o):
        greet(dev((x + o // 4) % 4, (y + o) % 4, c))

    greet(partner)

    @pl.loop(0, MATS)
    def _(i):
        load_g(i).start()

    def squares(i, total):
        load_g(i).wait()
        value = gbuf[i].astype(F32)
        return total + jnp.sum((value * value).reshape(ROWS // 8, 8, COLS), axis=0)

    total = lax.fori_loop(0, MATS, squares, jnp.zeros((8, COLS), F32))
    acc[0, 0:1] = jnp.sum(total, axis=0, keepdims=True)

    @pl.loop(0, MATS)
    def _(i):
        load_m(i).start()

    pl.semaphore_wait(barrier, 24)

    pl.semaphore_signal(relay.at[0], inc=1, device_id=(lax.rem(z + 4, 16), d), device_id_type=MESH)
    pl.semaphore_signal(relay.at[1], inc=1, device_id=(lax.rem(z + 12, 16), d), device_id_type=MESH)

    def core_copy():
        return remote(
            acc.at[0, pl.ds(0, 1)], accp.at[15, pl.ds(0, 1)], p_send.at[15], p_recv.at[15], partner
        )

    core_copy().start()
    core_copy().wait_recv()
    acc[1, 0:1] = acc[0, 0:1] + accp[15, 0:1]

    def p_copy(o):
        return remote(
            acc.at[1, pl.ds(0, 1)],
            accp.at[o - 1, pl.ds(0, 1)],
            p_send.at[o - 1],
            p_recv.at[o - 1],
            dev((x + o // 4) % 4, (y + o) % 4, c),
        )

    @pl.loop(1, 16)
    def _(o):
        p_copy(o).start()

    def gx_copy(j):
        return remote(gbuf.at[HALF * (1 - c) + j], gx.at[j], x_send.at[j], x_recv.at[j], partner)

    def mx_copy(j):
        return remote(mbuf.at[HALF * (1 - c) + j], mx.at[j], mx_send.at[j], mx_recv.at[j], partner)

    @pl.loop(0, MATS)
    def _(i):
        load_m(i).wait()

    @pl.loop(0, HALF)
    def _(j):
        @pl.when(HALF * (1 - c) + j < MATS)
        def _():
            gx_copy(j).start()
            mx_copy(j).start()

    pl.semaphore_wait(relay.at[0], 1)
    pl.semaphore_wait(relay.at[1], 1)

    @pl.loop(1, 16)
    def _(o):
        p_copy(o).wait_recv()

    acc[2, 0:1] = acc[1, 0:1] + jnp.sum(accp[0:15, 0:1, :], axis=0)

    def z_copy(o):
        return remote(
            acc.at[2, pl.ds(0, 1)],
            accz.at[o - 1, pl.ds(0, 1)],
            z_send.at[o - 1],
            z_recv.at[o - 1],
            (lax.rem(z + o, 16), d),
        )

    @pl.loop(1, 16)
    def _(o):
        z_copy(o).start()

    @pl.loop(1, 16)
    def _(o):
        z_copy(o).wait_recv()

    mean = jnp.sum(acc[2, 0:1] + jnp.sum(accz[:, 0:1, :], axis=0), keepdims=True) / ENTRIES + 1e-06
    root = lax.rsqrt(mean)
    root = root * (1.5 - 0.5 * mean * root * root)
    clip = jnp.minimum(1.0, root)

    def prepare(gradient, moment):
        scaled = gradient.astype(F32) * clip
        return (scaled + DECAY * (DECAY * moment + scaled)).astype(BF16)

    def owner(j):
        m = HALF * c + j
        return m < MATS, m % 4, (m // 4 + m % 4) % 4

    def slot(own, at):
        return jnp.maximum((own - at + 4) % 4 - 1, 0)

    def scale(px, py):
        return jnp.broadcast_to((16 + px * 4 + py).astype(F32) * 0.0625, (1, COLS))

    def s1_x(j, xm):
        k = slot(x, xm)
        return remote(
            gtx.at[j, pl.ds(0, PART)], r1.at[0, j, k], s1_send.at[0, j], s1_recv.at[0, j, k], dev(xm, y, c)
        )

    def s1_y(j, ym):
        k = slot(y, ym)
        return remote(
            gtx.at[j, pl.ds(PART, PART)], r1.at[1, j, k], s1_send.at[1, j], s1_recv.at[1, j, k], dev(x, ym, c)
        )

    @pl.loop(0, HALF)
    def _(j):
        real, xm, ym = owner(j)

        @pl.when(real)
        def _():
            m = HALF * c + j
            remote(gx.at[j], gx.at[j], x_send.at[j], x_recv.at[j], partner).wait_recv()
            remote(mx.at[j], mx.at[j], mx_send.at[j], mx_recv.at[j], partner).wait_recv()
            xx[j, 0] = prepare(gbuf[m], mbuf[m])
            xx[j, 1] = prepare(gx[j], mx[j])
            value = jnp.concatenate([xx[j, 0], xx[j, 1]], axis=1)
            top = dot_nt(value[:128], value[:256])
            mid = dot_nt(value[128:256], value[128:256])
            low = dot_nt(value[256:288], value)
            pieces = pack(top[:, :128], top[:, 128:], mid, low)
            own_scale = scale(x, y)
            for at, piece in pieces:
                gloc[j, at : at + piece.shape[0]] = piece
                gtx[j, at : at + piece.shape[0]] = (piece * own_scale).astype(BF16)

            @pl.when(xm != x)
            def _():
                s1_x(j, xm).start()

            @pl.when(ym != y)
            def _():
                s1_y(j, ym).start()

    def s2_x(j, ym):
        k = slot(y, ym)
        return remote(s2.at[0, j], r2.at[0, k], s2_send.at[0, j], s2_recv.at[0, k], dev(x, ym, c))

    def s2_y(j, xm):
        k = slot(x, xm)
        return remote(s2.at[1, j], r2.at[1, k], s2_send.at[1, j], s2_recv.at[1, k], dev(xm, y, c))

    def wait_r1(half, j, k):
        remote(r1.at[half, j, k], r1.at[half, j, k], s1_send.at[half, j], s1_recv.at[half, j, k], partner).wait_recv()

    def wait_r2(half, k):
        remote(r2.at[half, k], r2.at[half, k], s2_send.at[half, 0], s2_recv.at[half, k], partner).wait_recv()

    @pl.loop(0, HALF)
    def _(j):
        real, xm, ym = owner(j)

        def reduce(half, near, far, start):
            @pl.when(real & near)
            def _():
                for k in range(3):
                    wait_r1(half, j, k)
                total = gloc[j, PART * half : PART * half + PART]
                for k in range(3):
                    from_x = (x + k + 1) % 4 if half == 0 else x
                    from_y = y if half == 0 else (y + k + 1) % 4
                    total = total + r1[half, j, k].astype(F32) * (1.0 / scale(from_x, from_y))
                gloc[j, PART * half : PART * half + PART] = total

                @pl.when(far)
                def _():
                    s2[half, j] = (total * scale(x, y)).astype(BF16)
                    start()

        reduce(0, xm == x, ym != y, lambda: s2_x(j, ym).start())
        reduce(1, ym == y, xm != x, lambda: s2_y(j, xm).start())

    def q1_copy(j, half, k, o):
        target = dev(x, (y + o) % 4, c) if half == 0 else dev((x + o) % 4, y, c)
        return remote(
            qbuf.at[j, half, k], qbuf.at[j, half, k], q1_send.at[half, k, o - 1], q_recv.at[j, half, k], target
        )

    def q2_copy(j, half, k, o):
        target = dev((x + o) % 4, y, c) if half == 0 else dev(x, (y + o) % 4, c)
        return remote(
            qbuf.at[j, half, k], qbuf.at[j, half, k], q2_send.at[j, half, k, o - 1], q_recv.at[j, half, k], target
        )

    @pl.loop(0, HALF)
    def _(j):
        real, xm, ym = owner(j)

        @pl.when(real & (xm == x) & (ym == y))
        def _():
            for half in range(2):
                for k in range(3):
                    wait_r2(half, k)
                total = gloc[j, PART * half : PART * half + PART]
                for k in range(3):
                    from_x = x if half == 0 else (x + k + 1) % 4
                    from_y = (y + k + 1) % 4 if half == 0 else y
                    total = total + r2[half, k].astype(F32) * (1.0 / scale(from_x, from_y))
                gloc[j, PART * half : PART * half + PART] = total
            unpack(
                gf,
                gloc[j, 0:128],
                gloc[j, 128:256],
                gloc[j, 256:288],
                gloc[j, 288:320],
                gloc[j, 320:352],
            )
            row = lax.broadcasted_iota(jnp.int32, (ROWS, ROWS), 0)
            col = lax.broadcasted_iota(jnp.int32, (ROWS, ROWS), 1)
            diag = row == col
            raw = gf[...]
            norm = jnp.sqrt(jnp.sum(jnp.where(diag, raw, 0.0), keepdims=True)) + 1e-07
            inverse = 1.0 / norm
            gram = raw * (inverse * inverse)
            gram_s = split(gram)
            poly = TWO * gram + THREE * product(gram_s, gram_s) + jnp.where(diag, ONE, 0.0)
            poly_s = split(poly)
            left_s = split(product(poly_s, gram_s))
            gram = product(left_s, poly_s)
            gram_s = split(gram)
            last = TWO * gram + THREE * product(gram_s, gram_s) + jnp.where(diag, ONE, 0.0)
            gf[...] = product(split(last), poly_s) * (WIDTH_SCALE * inverse)

            pieces = pack(gf[0:128, 0:128], gf[0:128, 128:256], gf[128:256, 128:256], gf[256:288, :])
            for at, piece in pieces:
                both = split(piece)
                size = piece.shape[0]
                for half in range(2):
                    lo = max(at, PART * half)
                    hi = min(at + size, PART * half + PART)
                    if lo < hi:
                        for k in range(2):
                            qbuf[j, half, k, lo - PART * half : hi - PART * half] = both[k][lo - at : hi - at]
            for k in range(2):
                for half in range(2):
                    for o in (2, 1, 3):
                        q1_copy(j, half, k, o).start()

    def wait_q(j, half, k):
        remote(
            qbuf.at[j, half, k], qbuf.at[j, half, k], q1_send.at[half, k, 0], q_recv.at[j, half, k], partner
        ).wait_recv()

    for k in range(2):

        @pl.loop(0, HALF)
        def _(j):
            real, xm, ym = owner(j)

            def forward(half, near, far):
                @pl.when(real & near)
                def _():
                    @pl.when(far)
                    def _():
                        wait_q(j, half, k)

                    for o in (2, 1, 3):
                        q2_copy(j, half, k, o).start()

            forward(0, xm == x, ym != y)
            forward(1, ym == y, xm != x)

    @pl.loop(0, MATS)
    def _(i):
        nmbuf[i] = DECAY * mbuf[i] + gbuf[i].astype(F32) * clip
        store_nm(i).start()

    @pl.loop(0, MATS)
    def _(i):
        store_nm(i).wait()

    @pl.loop(1, 16)
    def _(o):
        z_copy(o).wait_send()
        p_copy(o).wait_send()

    core_copy().wait_send()

    @pl.loop(0, HALF)
    def _(j):
        real, xm, ym = owner(j)

        @pl.when(HALF * (1 - c) + j < MATS)
        def _():
            gx_copy(j).wait_send()
            mx_copy(j).wait_send()

        @pl.when(real)
        def _():
            @pl.when(xm != x)
            def _():
                s1_x(j, xm).wait_send()

            @pl.when(ym != y)
            def _():
                s1_y(j, ym).wait_send()

            @pl.when((xm == x) & (ym != y))
            def _():
                s2_x(j, ym).wait_send()

            @pl.when((ym == y) & (xm != x))
            def _():
                s2_y(j, xm).wait_send()

    def o_copy(j):
        m = HALF * c + j
        return remote(obuf.at[j, 1], o_hbm.at[m], o_send.at[j], o_recv.at[j], partner)

    def o_local(j):
        m = HALF * c + j
        return pltpu.make_async_copy(obuf.at[j, 0], o_hbm.at[m], ol_sem.at[j])

    @pl.loop(0, HALF)
    def _(j):
        real, xm, ym = owner(j)

        @pl.when(real)
        def _():
            @pl.when(xm != x)
            def _():
                wait_q(j, 0, 0)
                wait_q(j, 0, 1)

            @pl.when(ym != y)
            def _():
                wait_q(j, 1, 0)
                wait_q(j, 1, 1)

            first = qbuf[j, 0, 0].astype(F32) + qbuf[j, 0, 1].astype(F32)
            second = qbuf[j, 1, 0].astype(F32) + qbuf[j, 1, 1].astype(F32)
            cross = jnp.concatenate([first[128:176], second[0:80]], axis=0)
            unpack(gf, first[0:128], cross, second[80:112], second[112:144], second[144:176])
            full = split(gf[...])
            obuf[j, 1] = (dot(full[0], xx[j, 1]) + dot(full[1], xx[j, 1])).astype(BF16)
            o_copy(j).start()
            obuf[j, 0] = (dot(full[0], xx[j, 0]) + dot(full[1], xx[j, 0])).astype(BF16)
            o_local(j).start()

    @pl.loop(0, HALF)
    def _(j):
        real, xm, ym = owner(j)

        @pl.when(real & (xm == x) & (ym == y))
        def _():
            for k in range(2):
                for half in range(2):
                    for o in range(1, 4):
                        q1_copy(j, half, k, o).wait_send()

        @pl.when(real & (xm == x))
        def _():
            for k in range(2):
                for o in range(1, 4):
                    q2_copy(j, 0, k, o).wait_send()

        @pl.when(real & (ym == y))
        def _():
            for k in range(2):
                for o in range(1, 4):
                    q2_copy(j, 1, k, o).wait_send()

    @pl.loop(0, HALF)
    def _(j):
        @pl.when(HALF * (1 - c) + j < MATS)
        def _():
            remote(obuf.at[j, 1], obuf.at[j, 1], o_send.at[j], o_recv.at[j], partner).wait_recv()

        @pl.when(HALF * c + j < MATS)
        def _():
            o_local(j).wait()
            o_copy(j).wait_send()


def per_device(gradients, momentum):
    dma = pltpu.SemaphoreType.DMA
    vmem = pltpu.VMEM
    any_spec = pl.BlockSpec(memory_space=pl.ANY)
    return pl.pallas_call(
        kernel,
        out_shape=(
            jax.ShapeDtypeStruct((MATS, ROWS, COLS), F32),
            jax.ShapeDtypeStruct((MATS, ROWS, COLS), BF16),
        ),
        in_specs=[pl.BlockSpec(memory_space=pltpu.HBM)] * 2,
        out_specs=(any_spec, any_spec),
        scratch_shapes=[
            vmem((MATS, ROWS, COLS), BF16),
            vmem((MATS, ROWS, COLS), F32),
            vmem((MATS, ROWS, COLS), F32),
            vmem((3, 8, COLS), F32),
            vmem((15, 8, COLS), F32),
            vmem((16, 8, COLS), F32),
            vmem((HALF, ROWS, COLS), BF16),
            vmem((HALF, ROWS, COLS), F32),
            vmem((HALF, 2, ROWS, COLS), BF16),
            vmem((HALF, PACK, COLS), F32),
            vmem((HALF, PACK, COLS), BF16),
            vmem((2, HALF, 3, PART, COLS), BF16),
            vmem((2, HALF, PART, COLS), BF16),
            vmem((2, 3, PART, COLS), BF16),
            vmem((ROWS, ROWS), F32),
            vmem((HALF, 2, 2, PART, COLS), BF16),
            vmem((HALF, 2, ROWS, COLS), BF16),
            dma((MATS,)),
            dma((MATS,)),
            dma((MATS,)),
            dma((15,)),
            dma((15,)),
            dma((16,)),
            dma((16,)),
            dma((HALF,)),
            dma((HALF,)),
            dma((HALF,)),
            dma((HALF,)),
            dma((2, HALF)),
            dma((2, HALF, 3)),
            dma((2, HALF)),
            dma((2, 3)),
            dma((2, 2, 3)),
            dma((HALF, 2, 2, 3)),
            dma((HALF, 2, 2)),
            dma((HALF,)),
            dma((HALF,)),
            dma((HALF,)),
            pltpu.SemaphoreType.REGULAR((2,)),
        ],
        compiler_params=pltpu.CompilerParams(
            collective_id=0, has_side_effects=True, vmem_limit_bytes=40 * 1024 * 1024
        ),
        cost_estimate=pl.CostEstimate(flops=1500000000, bytes_accessed=5000000, transcendentals=0),
        name="muon",
    )(
        pltpu.with_memory_space_constraint(gradients, pltpu.HBM),
        pltpu.with_memory_space_constraint(momentum, pltpu.HBM),
    )


def solution(mesh):
    placed = (P("section", None, "dp"), P("section", None, "dp"))
    return jax.shard_map(
        per_device, mesh=mesh, in_specs=placed, out_specs=placed, check_vma=False
    )
```
